512 devices in a mesh: row: 4 (over z_lo), col: 16 (over x, z_hi), dp: 8 (over y, core).
Axes of the slice: x: 4, y: 4, z: 16 (z_hi: 4, z_lo: 4; z = z_hi * 4 + z_lo), core: 2. Of those that a mesh axis runs over, the one named last changes fastest.
Arguments:
- activations: bfloat16 [8, 2048, 12288], P('dp', 'row', 'col'), may hold values from -6 to 6
- out_grads: bfloat16 [8, 2048, 6144], P('dp', 'col', 'row'), may hold values from -0.046875 to 0.046875
Outputs:
- weight_grad: bfloat16 [12288, 6144], P(('col', 'dp'), 'row')
The draws below stay inside these ranges and needn't reach their ends.
All inputs are finite; a program needn't handle non-finite values.
Results may differ from the reference program's by a relative error of at most 0.017.
Values may be sent and summed in bfloat16 or wider, within the bound.
No kernel may reach another device: no remote copies, remote signals or barrier semaphores. Data moves between devices by JAX's collectives and lax.ppermute only.
A program may use at most 64 MiB of HBM per device.

```python
import jax
import jax.numpy as jnp
from jax import lax

D = 12288
DOUT = 6144
TOK = 2048
REPLICAS = 8


def spiked(drawn, stream_key, source, target, blocks, factor):
    owner, partner = [(jnp.arange(drawn.shape[dim]) // (drawn.shape[dim] // blocks)).reshape([-1 if axis == dim else 1 for axis in range(drawn.ndim)]) for dim in (source, target)]
    chosen = jax.random.permutation(stream_key, blocks)[partner]
    strong = (owner == chosen) | (owner == (partner + blocks // 2) % blocks)
    return jnp.where(strong, factor * drawn, drawn)


def shard_levels(rng, extent, shards, least, high):
    level = 1.0
    for axis_at, shards_of in shards:
        steps = jax.random.uniform(jax.random.fold_in(jax.random.fold_in(rng, 6), axis_at), (shards_of,), jnp.float32, least / len(shards), high / len(shards))
        level = level * jnp.repeat(jnp.exp(steps), extent[axis_at] // shards_of).reshape((-1,) + (1,) * (len(extent) - 1 - axis_at))
    return level


def centred(rng, extent, deviation, reach, split=(), dtype=jnp.bfloat16):
    array = jax.random.normal(rng, extent, jnp.float32) * deviation
    if len(split) > 0:
        array = shard_levels(rng, extent, split, -0.22, 0.18) * array
    return jnp.clip(array, min=-reach, max=reach).astype(dtype)


def bell_draw_with(stream_key, shape, spread, limit, pieces, heavy, held_as=jnp.bfloat16):
    array = spread * jax.random.normal(stream_key, shape, jnp.float32)
    if pieces:
        array = array * shard_levels(stream_key, shape, pieces, -0.22, 0.18)
    return jnp.clip(spiked(array, jax.random.fold_in(stream_key, 3), *heavy), -limit, limit).astype(held_as)


def setup_inputs(seed: int = 0) -> dict:
    key_of = jax.random.split(jax.random.key(seed), 3)
    return {
        "activations": bell_draw_with(key_of[0], (REPLICAS, TOK, D), 1.0, 6.0, ((0, 8), (1, 4), (2, 16)), (0, 2, 8, 2.0)),
        "out_grads": centred(key_of[1], (REPLICAS, TOK, DOUT), ((TOK * REPLICAS) ** -0.5), 0.046875, ((0, 8), (1, 16), (2, 4))),
    }


def reference(activations, out_grads):
    def add_replica(total, pair):
        inputs, grads = pair
        partial_value = jnp.dot(inputs.T, grads, preferred_element_type=jnp.float32).astype(jnp.bfloat16)
        partial_value = lax.optimization_barrier(partial_value)
        return total + partial_value.astype(jnp.float32), None

    start = jnp.zeros((activations.shape[2], out_grads.shape[2]), jnp.float32)
    total, _ = lax.scan(add_replica, start, (activations, out_grads))
    return total.astype(jnp.bfloat16)
```

```python
import jax
import jax.numpy as jnp
from jax import lax
from jax.experimental import pallas as pl
from jax.experimental.pallas import tpu as pltpu
from jax.sharding import PartitionSpec as P

F32, BF16 = jnp.float32, jnp.bfloat16
TILE = 256


def vmem_spec():
    return pl.BlockSpec(memory_space=pltpu.VMEM)


def smem_spec():
    return pl.BlockSpec(memory_space=pltpu.SMEM)


def any_spec():
    return pl.BlockSpec(memory_space=pl.ANY)


def params(mib):
    return pltpu.CompilerParams(vmem_limit_bytes=mib << 20)


def turn_kernel(where, a_ref, out_ref):
    h = where[2]
    for q in range(4):
        start = pl.multiple_of(lax.rem(h + q, 4) * 128, 128)
        out_ref[:, q * 128 : (q + 1) * 128] = a_ref[pl.ds(start, 128), :].T


def turn(where, a):
    return pl.pallas_call(
        turn_kernel,
        out_shape=jax.ShapeDtypeStruct((a.shape[1], a.shape[0]), BF16),
        in_specs=[smem_spec(), vmem_spec()],
        out_specs=vmem_spec(),
        compiler_params=params(16),
        name="turn",
    )(where, a)


def product_kernel(where, *refs):
    inputs, grads = refs[:6], refs[6:-7]
    other_ref, own_ref, left, right, total, in_sem, grad_sem = refs[-7:]
    line, x, core = where[0], where[1], where[4]
    started = []
    for t in range(4):
        delta = lax.rem(x + t, 4) - line
        place = left.at[:, pl.ds(t * 512, 512)]
        for source, test in zip(inputs, (
            delta == 0, delta == -1, delta == 1, delta == -2, delta == 2, jnp.abs(delta) == 3,
        )):
            @pl.when(test)
            def _():
                pltpu.make_async_copy(source, place, in_sem.at[t]).start()
        started.append(pltpu.make_async_copy(inputs[0], place, in_sem.at[t]))
    at = 0
    for i, source in enumerate(grads):
        copy = pltpu.make_async_copy(source, right.at[pl.ds(at, source.shape[0])], grad_sem.at[i])
        copy.start()
        started.append(copy)
        at += source.shape[0]
    for copy in started:
        copy.wait()

    def step(i, carry):
        columns = pl.ds(pl.multiple_of(i * TILE, TILE), TILE)
        total[:, columns] = jnp.dot(left[...], right[:, columns], preferred_element_type=F32)
        return carry

    lax.fori_loop(0, total.shape[1] // TILE, step, 0)
    for y in range(4):
        mine = pl.multiple_of(y * 192 + core * 96, 32)
        other = pl.multiple_of(y * 192 + (1 - core) * 96, 32)
        other_ref[y] = total[pl.ds(other, 96), :].astype(BF16)
        own_ref[y] = total[pl.ds(mine, 96), :]


def product(where, inputs, grads):
    rows, columns = inputs[0].shape[0], grads[0].shape[1]
    tokens = sum(g.shape[0] for g in grads)
    return pl.pallas_call(
        product_kernel,
        out_shape=[
            jax.ShapeDtypeStruct((4, rows // 8, columns), BF16),
            jax.ShapeDtypeStruct((4, rows // 8, columns), F32),
        ],
        in_specs=[smem_spec()] + [any_spec()] * (len(inputs) + len(grads)),
        out_specs=[vmem_spec(), vmem_spec()],
        scratch_shapes=[
            pltpu.VMEM((rows, tokens), BF16),
            pltpu.VMEM((tokens, columns), BF16),
            pltpu.VMEM((rows, columns), F32),
            pltpu.SemaphoreType.DMA((4,)),
            pltpu.SemaphoreType.DMA((len(grads),)),
        ],
        compiler_params=params(40),
        cost_estimate=pl.CostEstimate(flops=2 * rows * columns * tokens, bytes_accessed=12 << 20, transcendentals=0),
        name="product",
    )(where, *inputs, *grads)


def add_cores_kernel(where, own_ref, got_ref, *outs):
    y = where[3]
    for k in range(4):
        at = lax.rem(y + k, 4)
        outs[k][...] = (own_ref[at] + got_ref[at].astype(F32)).astype(outs[k].dtype)


def add_cores(where, own, got):
    shape = own.shape[1:]
    return pl.pallas_call(
        add_cores_kernel,
        out_shape=[jax.ShapeDtypeStruct(shape, F32)] + [jax.ShapeDtypeStruct(shape, BF16)] * 3,
        in_specs=[smem_spec(), vmem_spec(), vmem_spec()],
        out_specs=[vmem_spec()] * 4,
        compiler_params=params(16),
        name="add_cores",
    )(where, own, got)


def add_chips_kernel(kept_ref, *refs):
    total = kept_ref[...]
    for ref in refs[:-1]:
        total += ref[...].astype(F32)
    refs[-1][...] = total.astype(BF16)


def add_chips(kept, got):
    return pl.pallas_call(
        add_chips_kernel,
        out_shape=jax.ShapeDtypeStruct(kept.shape, BF16),
        in_specs=[vmem_spec()] * (1 + len(got)),
        out_specs=vmem_spec(),
        compiler_params=params(16),
        name="add_chips",
    )(kept, *got)


def along_x(value, step):
    return lax.ppermute(value, "col", [(x * 4 + h, (x + step) % 4 * 4 + h) for x in range(4) for h in range(4)])


def along_z_hi(value, step):
    return lax.ppermute(value, "col", [(x * 4 + h, x * 4 + (h + step) % 4) for x in range(4) for h in range(4)])


def along_row(value, pairs):
    return lax.ppermute(value, "row", pairs)


def along_y(value, step):
    return lax.ppermute(value, "dp", [(y * 2 + c, (y + step) % 4 * 2 + c) for y in range(4) for c in range(2)])


def shards(activations, out_grads):
    line, col, dp = lax.axis_index("row"), lax.axis_index("col"), lax.axis_index("dp")
    where = jnp.stack([line, col // 4, col % 4, dp // 2, dp % 2]).astype(jnp.int32)
    grads = out_grads[0]
    half = grads.shape[0] // 2

    before = along_z_hi(grads, 1)
    after = along_z_hi(grads, -1)
    own = turn(where, activations[0])
    from_low = along_row(own, [(0, 1), (1, 2), (2, 3)])
    from_high = along_row(own, [(3, 2), (2, 1), (1, 0)])
    far_top = along_z_hi(before[:half], 1)
    far_bottom = along_z_hi(after[half:], -1)
    near = jnp.concatenate([after, before])
    far = jnp.concatenate([far_top, far_bottom])
    low_2 = along_row(from_low, [(1, 2), (2, 3)])
    high_2 = along_row(from_high, [(2, 1), (1, 0)])
    ends = along_row(jnp.where(line == 2, low_2, high_2), [(2, 3), (1, 0)])

    pieces = []
    for t in range(4):
        sent = [grads, near, far] if t == 0 else [along_x(v, -t) for v in (grads, near, far)]
        pieces += [sent[0], sent[1][: 2 * half], sent[2], sent[1][2 * half :]]
    other, mine = product(where, [own, from_low, from_high, low_2, high_2, ends], pieces)
    got = lax.ppermute(other, "dp", [(d, d ^ 1) for d in range(8)])
    kept, *sends = add_cores(where, mine, got)
    return add_chips(kept, [along_y(v, k + 1) for k, v in enumerate(sends)])


def solution(mesh):
    in_specs = (P("dp", "row", "col"), P("dp", "col", "row"))
    out_specs = P(("col", "dp"), "row")
    return jax.shard_map(shards, mesh=mesh, in_specs=in_specs, out_specs=out_specs, check_vma=False)
```

```python
import jax
import jax.numpy as jnp
from jax import lax
from jax.experimental import pallas as pl
from jax.experimental.pallas import tpu as pltpu
from jax.sharding import Mesh, PartitionSpec as P

F32, BF16 = jnp.float32, jnp.bfloat16
TILE = 256
CHUNK = 512


def vmem_spec():
    return pl.BlockSpec(memory_space=pltpu.VMEM)


def smem_spec():
    return pl.BlockSpec(memory_space=pltpu.SMEM)


def hbm_spec():
    return pl.BlockSpec(memory_space=pltpu.HBM)


def params(mib):
    return pltpu.CompilerParams(vmem_limit_bytes=mib << 20)


def turn_kernel(where, a_ref, out_ref):
    h = where[2]
    for q, ahead in enumerate((0, 1, 3, 2)):
        start = pl.multiple_of(lax.rem(h + ahead, 4) * 128, 128)
        out_ref[:, q * 128 : (q + 1) * 128] = a_ref[pl.ds(start, 128), :].T


def turn(where, a):
    return pl.pallas_call(
        turn_kernel,
        out_shape=jax.ShapeDtypeStruct((a.shape[1], a.shape[0]), BF16),
        in_specs=[smem_spec(), vmem_spec()],
        out_specs=vmem_spec(),
        compiler_params=params(16),
        name="turn",
    )(where, a)


def load_grads(x, chunk, refs, place, sems, start):
    own_ref, near_ref, *far_refs = refs
    own_at, near_at, far_at = (place.at[pl.ds(at, size)] for at, size in ((0, 128), (128, 256), (384, 128)))
    if start:
        pltpu.make_async_copy(own_ref.at[chunk], own_at, sems.at[0]).start()
        pltpu.make_async_copy(near_ref.at[chunk], near_at, sems.at[1]).start()
        for t, ref in enumerate(far_refs):
            pl.when(lax.rem(x + t, 4) == chunk)(pltpu.make_async_copy(ref, far_at, sems.at[2]).start)
    else:
        pltpu.make_async_copy(own_ref.at[chunk], own_at, sems.at[0]).wait()
        pltpu.make_async_copy(near_ref.at[chunk], near_at, sems.at[1]).wait()
        pltpu.make_async_copy(far_refs[0], far_at, sems.at[2]).wait()


def early_kernel(where, own_ref, low_ref, high_ref, *refs):
    grads, (total_ref, rest_ref, left, right, in_sem, grad_sem, rest_sem) = refs[:6], refs[6:]
    line = where[0]
    steps = (
        (own_ref, line, None),
        (low_ref, line - 1, line > 0),
        (high_ref, line + 1, line < 3),
    )
    columns = total_ref.shape[1]

    def run(test, body):
        body() if test is None else pl.when(test)(body)

    for i, (source, chunk, test) in enumerate(steps):
        def begin():
            pltpu.make_async_copy(source, left.at[i], in_sem.at[i]).start()
            load_grads(where[1], chunk, grads, right.at[i], grad_sem.at[i], True)
        run(test, begin)
    rest = (lax.rem(line + 2, 4), 3 - line)
    for i, chunk in enumerate(rest):
        load_grads(where[1], chunk, grads, rest_ref.at[i], rest_sem.at[i], True)
    for i, (source, chunk, test) in enumerate(steps):
        def multiply():
            pltpu.make_async_copy(source, left.at[i], in_sem.at[i]).wait()
            load_grads(where[1], chunk, grads, right.at[i], grad_sem.at[i], False)

            def step(j, carry):
                at = pl.ds(pl.multiple_of(j * TILE, TILE), TILE)
                value = jnp.dot(left[i], right[i, :, at], preferred_element_type=F32)
                total_ref[:, at] = value if i == 0 else total_ref[:, at] + value
                return carry

            lax.fori_loop(0, columns // TILE, step, 0)
        run(test, multiply)
    for i, chunk in enumerate(rest):
        load_grads(where[1], chunk, grads, rest_ref.at[i], rest_sem.at[i], False)


def early(where, own, low, high, own_grads, near_grads, far_grads):
    rows, columns = own.shape[0], own_grads.shape[-1]
    return pl.pallas_call(
        early_kernel,
        out_shape=[
            jax.ShapeDtypeStruct((rows, columns), F32),
            jax.ShapeDtypeStruct((2, CHUNK, columns), BF16),
        ],
        in_specs=[smem_spec()] + [hbm_spec()] * 9,
        out_specs=[vmem_spec(), vmem_spec()],
        scratch_shapes=[
            pltpu.VMEM((3, rows, CHUNK), BF16),
            pltpu.VMEM((3, CHUNK, columns), BF16),
            pltpu.SemaphoreType.DMA((3,)),
            pltpu.SemaphoreType.DMA((3, 3)),
            pltpu.SemaphoreType.DMA((2, 3)),
        ],
        compiler_params=params(32),
        cost_estimate=pl.CostEstimate(flops=6 * rows * columns * CHUNK, bytes_accessed=16 << 20, transcendentals=0),
        name="early",
    )(where, own, low, high, own_grads, near_grads, *far_grads)


def late_kernel(where, total_ref, rest_ref, low_ref, high_ref, ends_ref, other_ref, own_ref, left, in_sem):
    line, core = where[0], where[4]
    at_end = jnp.logical_or(line == 0, line == 3)

    @pl.when(line >= 2)
    def _():
        pltpu.make_async_copy(low_ref, left.at[:, pl.ds(0, CHUNK)], in_sem.at[0]).start()

    @pl.when(line < 2)
    def _():
        pltpu.make_async_copy(high_ref, left.at[:, pl.ds(0, CHUNK)], in_sem.at[0]).start()

    end_copy = pltpu.make_async_copy(ends_ref, left.at[:, pl.ds(CHUNK, CHUNK)], in_sem.at[1])
    pl.when(at_end)(end_copy.start)
    pltpu.make_async_copy(low_ref, left.at[:, pl.ds(0, CHUNK)], in_sem.at[0]).wait()
    share = other_ref.shape[1]

    def add(chunks):
        def step(j, carry):
            at = pl.ds(pl.multiple_of(j * TILE, TILE), TILE)
            right = jnp.concatenate([rest_ref[i, :, at] for i in range(chunks)])
            value = total_ref[:, at] + jnp.dot(left[:, : chunks * CHUNK], right, preferred_element_type=F32)
            for y in range(4):
                even = value[2 * y * share : (2 * y + 1) * share]
                odd = value[(2 * y + 1) * share : (2 * y + 2) * share]
                own_ref[y, :, at] = jnp.where(core == 0, even, odd)
                other_ref[y, :, at] = jnp.where(core == 0, odd, even).astype(BF16)
            return carry

        lax.fori_loop(0, total_ref.shape[1] // TILE, step, 0)

    @pl.when(at_end)
    def _():
        end_copy.wait()
        add(2)

    @pl.when(jnp.logical_not(at_end))
    def _():
        add(1)


def late(where, total, rest, low, high, ends):
    rows, columns = total.shape
    return pl.pallas_call(
        late_kernel,
        out_shape=[
            jax.ShapeDtypeStruct((4, rows // 8, columns), BF16),
            jax.ShapeDtypeStruct((4, rows // 8, columns), F32),
        ],
        in_specs=[smem_spec(), vmem_spec(), vmem_spec()] + [hbm_spec()] * 3,
        out_specs=[vmem_spec(), vmem_spec()],
        scratch_shapes=[pltpu.VMEM((rows, 2 * CHUNK), BF16), pltpu.SemaphoreType.DMA((2,))],
        compiler_params=params(32),
        cost_estimate=pl.CostEstimate(flops=4 * rows * columns * CHUNK, bytes_accessed=8 << 20, transcendentals=0),
        name="late",
    )(where, total, rest, low, high, ends)


def add_cores_kernel(where, own_ref, got_ref, *outs):
    y = where[3]
    for k in range(4):
        at = lax.rem(y + k, 4)
        outs[k][...] = (own_ref[at] + got_ref[at].astype(F32)).astype(outs[k].dtype)


def add_cores(where, own, got):
    shape = own.shape[1:]
    return pl.pallas_call(
        add_cores_kernel,
        out_shape=[jax.ShapeDtypeStruct(shape, F32)] + [jax.ShapeDtypeStruct(shape, BF16)] * 3,
        in_specs=[smem_spec(), vmem_spec(), vmem_spec()],
        out_specs=[vmem_spec()] * 4,
        compiler_params=params(16),
        name="add_cores",
    )(where, own, got)


def add_chips_kernel(kept_ref, *refs):
    total = kept_ref[...]
    for ref in refs[:-1]:
        total += ref[...].astype(F32)
    refs[-1][...] = total.astype(BF16)


def add_chips(kept, got):
    return pl.pallas_call(
        add_chips_kernel,
        out_shape=jax.ShapeDtypeStruct(kept.shape, BF16),
        in_specs=[vmem_spec()] * (1 + len(got)),
        out_specs=vmem_spec(),
        compiler_params=params(16),
        name="add_chips",
    )(kept, *got)


def ring(value, axis, step):
    return lax.ppermute(value, axis, [(i, (i + step) % 4) for i in range(4)])


def shards(activations, out_grads):
    where = jnp.stack([lax.axis_index(n) for n in ("row", "x", "z_hi", "y", "core")]).astype(jnp.int32)
    line = where[0]
    grads = out_grads[0]
    half = grads.shape[0] // 2

    own_grads = lax.all_gather(grads, "x", axis=0)
    own = turn(where, activations[0])
    before = ring(grads, "z_hi", 1)
    after = ring(grads, "z_hi", -1)
    near = jnp.concatenate([after, before])
    near, top, bottom, own = lax.optimization_barrier((near, before[:half], after[half:], own))
    near_grads = lax.all_gather(near, "x", axis=0)

    far_top = ring(top, "z_hi", 1)
    far_bottom = ring(bottom, "z_hi", -1)
    low_1 = lax.ppermute(own, "row", [(0, 1), (1, 2), (2, 3)])
    high_1 = lax.ppermute(own, "row", [(3, 2), (2, 1), (1, 0)])
    far = jnp.concatenate([far_top, far_bottom])
    sent_on = jnp.where(line == 1, low_1, high_1)
    far, low_1, high_1, sent_on = lax.optimization_barrier((far, low_1, high_1, sent_on))

    ends = lax.ppermute(sent_on, "row", [(1, 3), (2, 0)])
    low_2 = lax.ppermute(low_1, "row", [(1, 2), (2, 3)])
    high_2 = lax.ppermute(high_1, "row", [(2, 1), (1, 0)])
    far_grads = [ring(far, "x", -t) for t in (2, 1, 3)]
    far_grads = [far, far_grads[1], far_grads[0], far_grads[2]]

    total, rest = early(where, own, low_1, high_1, own_grads, near_grads, far_grads)
    other, mine = late(where, total, rest, low_2, high_2, ends)
    got = lax.ppermute(other, "core", [(0, 1), (1, 0)])
    kept, *sends = add_cores(where, mine, got)
    return add_chips(kept, [ring(v, "y", k + 1) for k, v in enumerate(sends)])


def solution(mesh):
    parts = Mesh(mesh.devices.reshape(4, 4, 4, 4, 2), ("row", "x", "z_hi", "y", "core"))
    in_specs = (P(("y", "core"), "row", ("x", "z_hi")), P(("y", "core"), ("x", "z_hi"), "row"))
    out_specs = P(("x", "z_hi", "y", "core"), "row")
    return jax.shard_map(shards, mesh=parts, in_specs=in_specs, out_specs=out_specs, check_vma=False)
```

```python
import jax
import jax.numpy as jnp
from jax import lax
from jax.experimental import pallas as pl
from jax.experimental.pallas import tpu as pltpu
from jax.sharding import Mesh, PartitionSpec as P

F32, BF16 = jnp.float32, jnp.bfloat16
TILE = 512
CHUNK = 512


def vmem_spec():
    return pl.BlockSpec(memory_space=pltpu.VMEM)


def smem_spec():
    return pl.BlockSpec(memory_space=pltpu.SMEM)


def any_spec():
    return pl.BlockSpec(memory_space=pl.ANY)


def params(mib):
    return pltpu.CompilerParams(vmem_limit_bytes=mib << 20)


def turn_kernel(where, a_ref, out_ref, turned):
    h, core = where[2], where[4]
    share = out_ref.shape[0] // 8
    for q, ahead in enumerate((0, 1, 3, 2)):
        start = pl.multiple_of(lax.rem(h + ahead, 4) * 128, 128)
        turned[:, q * 128 : (q + 1) * 128] = a_ref[pl.ds(start, 128), :].T
    for y in range(4):
        for i, keeper in enumerate((1 - core, core)):
            at = pl.multiple_of((2 * y + keeper) * share, 32)
            out_ref[(4 * i + y) * share : (4 * i + y + 1) * share, :] = turned[pl.ds(at, share), :]


def turn(where, a):
    shape = (a.shape[1], a.shape[0])
    return pl.pallas_call(
        turn_kernel,
        out_shape=jax.ShapeDtypeStruct(shape, BF16),
        in_specs=[smem_spec(), vmem_spec()],
        out_specs=vmem_spec(),
        scratch_shapes=[pltpu.VMEM(shape, BF16)],
        compiler_params=params(16),
        name="turn",
    )(where, a)


def stage_kernel(*refs):
    pieces, (out_ref, sems) = refs[:-2], refs[-2:]
    at, copies = 0, []
    for i, ref in enumerate(pieces):
        copies.append(pltpu.make_async_copy(ref, out_ref.at[pl.ds(at, ref.shape[0])], sems.at[i]))
        at += ref.shape[0]
    for copy in copies:
        copy.start()
    for copy in copies:
        copy.wait()


def stage(pieces):
    tokens = sum(p.shape[0] for p in pieces)
    return pl.pallas_call(
        stage_kernel,
        out_shape=jax.ShapeDtypeStruct((tokens, pieces[0].shape[1]), BF16),
        in_specs=[any_spec()] * len(pieces),
        out_specs=vmem_spec(),
        scratch_shapes=[pltpu.SemaphoreType.DMA((len(pieces),))],
        compiler_params=params(54),
        cost_estimate=pl.CostEstimate(flops=0, bytes_accessed=12 << 20, transcendentals=0),
        name="stage",
    )(*pieces)


def product_kernel(where, a_ref, right_ref, other_ref, own_ref, left, sems):
    copies = []
    for t in range(4):
        chunk = lax.rem(where[1] + t, 4)
        copies.append(pltpu.make_async_copy(a_ref.at[chunk], left.at[:, pl.ds(t * CHUNK, CHUNK)], sems.at[t]))
    for copy in copies:
        copy.start()
    for copy in copies:
        copy.wait()
    share = other_ref.shape[1]

    def step(j, carry):
        at = pl.ds(pl.multiple_of(j * TILE, TILE), TILE)
        value = jnp.dot(left[...], right_ref[:, at], preferred_element_type=F32)
        for y in range(4):
            other_ref[y, :, at] = value[y * share : (y + 1) * share].astype(BF16)
            own_ref[y, :, at] = value[(4 + y) * share : (5 + y) * share]
        return carry

    lax.fori_loop(0, right_ref.shape[1] // TILE, step, 0)


def product(where, inputs, right):
    rows, (tokens, columns) = inputs.shape[1], right.shape
    return pl.pallas_call(
        product_kernel,
        out_shape=[
            jax.ShapeDtypeStruct((4, rows // 8, columns), BF16),
            jax.ShapeDtypeStruct((4, rows // 8, columns), F32),
        ],
        in_specs=[smem_spec(), any_spec(), vmem_spec()],
        out_specs=[vmem_spec(), vmem_spec()],
        scratch_shapes=[pltpu.VMEM((rows, tokens), BF16), pltpu.SemaphoreType.DMA((4,))],
        compiler_params=params(50),
        cost_estimate=pl.CostEstimate(flops=2 * rows * columns * tokens, bytes_accessed=10 << 20, transcendentals=0),
        name="product",
    )(where, inputs, right)


def add_cores_kernel(where, own_ref, got_ref, *outs):
    y = where[3]
    for k in range(4):
        at = lax.rem(y + k, 4)
        outs[k][...] = (own_ref[at] + got_ref[at].astype(F32)).astype(outs[k].dtype)


def add_cores(where, own, got):
    shape = own.shape[1:]
    return pl.pallas_call(
        add_cores_kernel,
        out_shape=[jax.ShapeDtypeStruct(shape, F32)] + [jax.ShapeDtypeStruct(shape, BF16)] * 3,
        in_specs=[smem_spec(), vmem_spec(), vmem_spec()],
        out_specs=[vmem_spec()] * 4,
        compiler_params=params(16),
        name="add_cores",
    )(where, own, got)


def add_chips_kernel(kept_ref, *refs):
    total = kept_ref[...]
    for ref in refs[:-1]:
        total += ref[...].astype(F32)
    refs[-1][...] = total.astype(BF16)


def add_chips(kept, got):
    return pl.pallas_call(
        add_chips_kernel,
        out_shape=jax.ShapeDtypeStruct(kept.shape, BF16),
        in_specs=[vmem_spec()] * (1 + len(got)),
        out_specs=vmem_spec(),
        compiler_params=params(16),
        name="add_chips",
    )(kept, *got)


def ring(value, axis, step):
    return lax.ppermute(value, axis, [(i, (i + step) % 4) for i in range(4)])


def shards(activations, out_grads):
    where = jnp.stack([lax.axis_index(n) for n in ("row", "x", "z_hi", "y", "core")]).astype(jnp.int32)
    grads = out_grads[0]
    half = grads.shape[0] // 2

    inputs = lax.all_gather(turn(where, activations[0]), "row", axis=0)

    before = ring(grads, "z_hi", 1)
    after = ring(grads, "z_hi", -1)
    owns = [ring(grads, "x", -t) for t in (1, 2, 3)]
    near = jnp.concatenate([after, before])
    near, top, bottom, *owns = lax.optimization_barrier((near, before[:half], after[half:], *owns))

    far_top = ring(top, "z_hi", 1)
    far_bottom = ring(bottom, "z_hi", -1)
    nears = [ring(near, "x", -t) for t in (1, 2, 3)]
    far_top, far_bottom, *nears = lax.optimization_barrier((far_top, far_bottom, *nears))

    far = jnp.concatenate([far_top, far_bottom])
    fars = [ring(far, "x", -t) for t in (1, 2, 3)]

    right = stage([grads, near, far] + [p for group in zip(owns, nears, fars) for p in group])
    other, mine = product(where, inputs, right)
    got = lax.ppermute(other, "core", [(0, 1), (1, 0)])
    kept, *sends = add_cores(where, mine, got)
    return add_chips(kept, [ring(sends[k - 1], "y", k) for k in (2, 1, 3)])


def solution(mesh):
    parts = Mesh(mesh.devices.reshape(4, 4, 4, 4, 2), ("row", "x", "z_hi", "y", "core"))
    in_specs = (P(("y", "core"), "row", ("x", "z_hi")), P(("y", "core"), ("x", "z_hi"), "row"))
    out_specs = P(("x", "z_hi", "y", "core"), "row")
    return jax.shard_map(shards, mesh=parts, in_specs=in_specs, out_specs=out_specs, check_vma=False)
```

```python
import jax
import jax.numpy as jnp
from jax import lax
from jax.experimental import pallas as pl
from jax.experimental.pallas import tpu as pltpu
from jax.sharding import Mesh, PartitionSpec as P

F32, BF16 = jnp.float32, jnp.bfloat16
TILE = 512
CHUNK = 512


def vmem_spec():
    return pl.BlockSpec(memory_space=pltpu.VMEM)


def smem_spec():
    return pl.BlockSpec(memory_space=pltpu.SMEM)


def any_spec():
    return pl.BlockSpec(memory_space=pl.ANY)


def params(mib):
    return pltpu.CompilerParams(vmem_limit_bytes=mib << 20)


def turn_kernel(where, a_ref, out_ref, turned):
    h, core = where[2], where[4]
    share = out_ref.shape[0] // 8
    for q, ahead in enumerate((0, 1, 3, 2)):
        start = pl.multiple_of(lax.rem(h + ahead, 4) * 128, 128)
        turned[:, q * 128 : (q + 1) * 128] = a_ref[pl.ds(start, 128), :].T
    for y in range(4):
        for i, keeper in enumerate((1 - core, core)):
            at = pl.multiple_of((2 * y + keeper) * share, 32)
            out_ref[(4 * i + y) * share : (4 * i + y + 1) * share, :] = turned[pl.ds(at, share), :]


def turn(where, a):
    shape = (a.shape[1], a.shape[0])
    return pl.pallas_call(
        turn_kernel,
        out_shape=jax.ShapeDtypeStruct(shape, BF16),
        in_specs=[smem_spec(), vmem_spec()],
        out_specs=vmem_spec(),
        scratch_shapes=[pltpu.VMEM(shape, BF16)],
        compiler_params=params(16),
        name="turn",
    )(where, a)


def stage_kernel(*refs):
    pieces, (out_ref, sems) = refs[:-2], refs[-2:]
    at, copies = 0, []
    for i, ref in enumerate(pieces):
        copies.append(pltpu.make_async_copy(ref, out_ref.at[pl.ds(at, ref.shape[0])], sems.at[i]))
        at += ref.shape[0]
    for copy in copies:
        copy.start()
    for copy in copies:
        copy.wait()


def stage(pieces):
    tokens = sum(p.shape[0] for p in pieces)
    return pl.pallas_call(
        stage_kernel,
        out_shape=jax.ShapeDtypeStruct((tokens, pieces[0].shape[1]), BF16),
        in_specs=[any_spec()] * len(pieces),
        out_specs=vmem_spec(),
        scratch_shapes=[pltpu.SemaphoreType.DMA((len(pieces),))],
        compiler_params=params(54),
        cost_estimate=pl.CostEstimate(flops=0, bytes_accessed=12 << 20, transcendentals=0),
        name="stage",
    )(*pieces)


def product_kernel(where, a_ref, right_ref, other_ref, own_ref, left, sems):
    copies = []
    for t in range(4):
        chunk = lax.rem(where[1] + t, 4)
        copies.append(pltpu.make_async_copy(a_ref.at[chunk], left.at[:, pl.ds(t * CHUNK, CHUNK)], sems.at[t]))
    for copy in copies:
        copy.start()
    for copy in copies:
        copy.wait()
    share = other_ref.shape[1]

    def step(j, carry):
        at = pl.ds(pl.multiple_of(j * TILE, TILE), TILE)
        value = jnp.dot(left[...], right_ref[:, at], preferred_element_type=F32)
        for y in range(4):
            other_ref[y, :, at] = value[y * share : (y + 1) * share].astype(BF16)
            own_ref[y, :, at] = value[(4 + y) * share : (5 + y) * share].astype(BF16)
        return carry

    lax.fori_loop(0, right_ref.shape[1] // TILE, step, 0)


def product(where, inputs, right):
    rows, (tokens, columns) = inputs.shape[1], right.shape
    return pl.pallas_call(
        product_kernel,
        out_shape=[
            jax.ShapeDtypeStruct((4, rows // 8, columns), BF16),
            jax.ShapeDtypeStruct((4, rows // 8, columns), BF16),
        ],
        in_specs=[smem_spec(), any_spec(), vmem_spec()],
        out_specs=[vmem_spec(), vmem_spec()],
        scratch_shapes=[pltpu.VMEM((rows, tokens), BF16), pltpu.SemaphoreType.DMA((4,))],
        compiler_params=params(50),
        cost_estimate=pl.CostEstimate(flops=2 * rows * columns * tokens, bytes_accessed=10 << 20, transcendentals=0),
        name="product",
    )(where, inputs, right)


def add_cores_kernel(where, own_ref, got_ref, *outs):
    y = where[3]
    for k in range(4):
        at = lax.rem(y + k, 4)
        outs[k][...] = (own_ref[at].astype(F32) + got_ref[at].astype(F32)).astype(outs[k].dtype)


def add_cores(where, own, got):
    shape = own.shape[1:]
    return pl.pallas_call(
        add_cores_kernel,
        out_shape=[jax.ShapeDtypeStruct(shape, F32)] + [jax.ShapeDtypeStruct(shape, BF16)] * 3,
        in_specs=[smem_spec(), vmem_spec(), vmem_spec()],
        out_specs=[vmem_spec()] * 4,
        compiler_params=params(16),
        name="add_cores",
    )(where, own, got)


def add_chips_kernel(kept_ref, *refs):
    total = kept_ref[...]
    for ref in refs[:-1]:
        total += ref[...].astype(F32)
    refs[-1][...] = total.astype(BF16)


def add_chips(kept, got):
    return pl.pallas_call(
        add_chips_kernel,
        out_shape=jax.ShapeDtypeStruct(kept.shape, BF16),
        in_specs=[vmem_spec()] * (1 + len(got)),
        out_specs=vmem_spec(),
        compiler_params=params(16),
        name="add_chips",
    )(kept, *got)


def ring(value, axis, step):
    return lax.ppermute(value, axis, [(i, (i + step) % 4) for i in range(4)])


def shards(activations, out_grads):
    where = jnp.stack([lax.axis_index(n) for n in ("row", "x", "z_hi", "y", "core")]).astype(jnp.int32)
    grads = out_grads[0]
    half = grads.shape[0] // 2

    turned = turn(where, activations[0])
    before = ring(grads, "z_hi", 1)
    after = ring(grads, "z_hi", -1)
    owns = [ring(grads, "x", -t) for t in (1, 2, 3)]
    near = jnp.concatenate([after, before])
    near, top, bottom, turned, *owns = lax.optimization_barrier((near, before[:half], after[half:], turned, *owns))

    inputs = lax.all_gather(turned, "row", axis=0)

    far_top = ring(top, "z_hi", 1)
    far_bottom = ring(bottom, "z_hi", -1)
    nears = [ring(near, "x", -t) for t in (1, 2, 3)]
    far_top, far_bottom, *nears = lax.optimization_barrier((far_top, far_bottom, *nears))

    far = jnp.concatenate([far_top, far_bottom])
    fars = [ring(far, "x", -t) for t in (1, 2, 3)]

    right = stage([grads, near, far] + [p for group in zip(owns, nears, fars) for p in group])
    other, mine = product(where, inputs, right)
    got = lax.ppermute(other, "core", [(0, 1), (1, 0)])
    kept, *sends = add_cores(where, mine, got)
    return add_chips(kept, [ring(sends[k - 1], "y", k) for k in (2, 1, 3)])


def solution(mesh):
    parts = Mesh(mesh.devices.reshape(4, 4, 4, 4, 2), ("row", "x", "z_hi", "y", "core"))
    in_specs = (P(("y", "core"), "row", ("x", "z_hi")), P(("y", "core"), ("x", "z_hi"), "row"))
    out_specs = P(("x", "z_hi", "y", "core"), "row")
    return jax.shard_map(shards, mesh=parts, in_specs=in_specs, out_specs=out_specs, check_vma=False)
```

```python
import jax
import jax.numpy as jnp
from jax import lax
from jax.experimental import pallas as pl
from jax.experimental.pallas import tpu as pltpu
from jax.sharding import Mesh, PartitionSpec as P

F32, BF16 = jnp.float32, jnp.bfloat16
CHUNK = 512


def vmem_spec():
    return pl.BlockSpec(memory_space=pltpu.VMEM)


def smem_spec():
    return pl.BlockSpec(memory_space=pltpu.SMEM)


def any_spec():
    return pl.BlockSpec(memory_space=pl.ANY)


def params(mib):
    return pltpu.CompilerParams(vmem_limit_bytes=mib << 20)


def turn_kernel(where, a_ref, out_ref, turned):
    h, core = where[2], where[4]
    share = out_ref.shape[0] // 8
    for q, ahead in enumerate((0, 1, 3, 2)):
        start = pl.multiple_of(lax.rem(h + ahead, 4) * 128, 128)
        turned[:, q * 128 : (q + 1) * 128] = a_ref[pl.ds(start, 128), :].T
    for y in range(4):
        for i, keeper in enumerate((1 - core, core)):
            at = pl.multiple_of((2 * y + keeper) * share, 32)
            out_ref[(4 * i + y) * share : (4 * i + y + 1) * share, :] = turned[pl.ds(at, share), :]


def turn(where, a):
    shape = (a.shape[1], a.shape[0])
    return pl.pallas_call(
        turn_kernel,
        out_shape=jax.ShapeDtypeStruct(shape, BF16),
        in_specs=[smem_spec(), vmem_spec()],
        out_specs=vmem_spec(),
        scratch_shapes=[pltpu.VMEM(shape, BF16)],
        compiler_params=params(16),
        name="turn",
    )(where, a)


def stage_kernel(*refs):
    pieces, (out_ref, sems) = refs[:-2], refs[-2:]
    at, copies = 0, []
    for i, ref in enumerate(pieces):
        copies.append(pltpu.make_async_copy(ref, out_ref.at[pl.ds(at, ref.shape[0])], sems.at[i]))
        at += ref.shape[0]
    for copy in copies:
        copy.start()
    for copy in copies:
        copy.wait()


def stage(pieces):
    tokens = sum(p.shape[0] for p in pieces)
    return pl.pallas_call(
        stage_kernel,
        out_shape=jax.ShapeDtypeStruct((tokens, pieces[0].shape[1]), BF16),
        in_specs=[any_spec()] * len(pieces),
        out_specs=vmem_spec(),
        scratch_shapes=[pltpu.SemaphoreType.DMA((len(pieces),))],
        compiler_params=params(54),
        cost_estimate=pl.CostEstimate(flops=0, bytes_accessed=12 << 20, transcendentals=0),
        name="stage",
    )(*pieces)


def product_kernel(where, a_ref, grads_ref, other_ref, own_ref, left, right, total, sems):
    waits = []
    for t in range(4):
        chunk = lax.rem(where[1] + t, 4)
        here = pl.ds(t * CHUNK, CHUNK)
        waits.append([
            pltpu.make_async_copy(a_ref.at[chunk], left.at[:, here], sems.at[t, 0]),
            pltpu.make_async_copy(grads_ref.at[here], right.at[here], sems.at[t, 1]),
        ])
    for copies in waits:
        for copy in copies:
            copy.start()
    share = other_ref.shape[1]
    for first, last in ((0, 1), (1, 2), (2, 4)):
        for copies in waits[first:last]:
            for copy in copies:
                copy.wait()
        across = slice(first * CHUNK, last * CHUNK)
        value = jnp.dot(left[:, across], right[across, :], preferred_element_type=F32)
        if first > 0:
            value = total[...] + value
        if last < 4:
            total[...] = value
        else:
            for y in range(4):
                other_ref[y] = value[y * share : (y + 1) * share].astype(BF16)
                own_ref[y] = value[(4 + y) * share : (5 + y) * share].astype(BF16)


def product(where, inputs, grads):
    rows, (tokens, columns) = inputs.shape[1], grads.shape
    return pl.pallas_call(
        product_kernel,
        out_shape=[jax.ShapeDtypeStruct((4, rows // 8, columns), BF16)] * 2,
        in_specs=[smem_spec(), any_spec(), any_spec()],
        out_specs=[vmem_spec(), vmem_spec()],
        scratch_shapes=[
            pltpu.VMEM((rows, tokens), BF16),
            pltpu.VMEM((tokens, columns), BF16),
            pltpu.VMEM((rows, columns), F32),
            pltpu.SemaphoreType.DMA((4, 2)),
        ],
        compiler_params=params(50),
        cost_estimate=pl.CostEstimate(flops=2 * rows * columns * tokens, bytes_accessed=12 << 20, transcendentals=0),
        name="product",
    )(where, inputs, grads)


def add_cores_kernel(where, own_ref, got_ref, *outs):
    y = where[3]
    for k in range(4):
        at = lax.rem(y + k, 4)
        outs[k][...] = (own_ref[at].astype(F32) + got_ref[at].astype(F32)).astype(outs[k].dtype)


def add_cores(where, own, got):
    shape = own.shape[1:]
    return pl.pallas_call(
        add_cores_kernel,
        out_shape=[jax.ShapeDtypeStruct(shape, F32)] + [jax.ShapeDtypeStruct(shape, BF16)] * 3,
        in_specs=[smem_spec(), vmem_spec(), vmem_spec()],
        out_specs=[vmem_spec()] * 4,
        compiler_params=params(16),
        name="add_cores",
    )(where, own, got)


def add_chips_kernel(kept_ref, *refs):
    total = kept_ref[...]
    for ref in refs[:-1]:
        total += ref[...].astype(F32)
    refs[-1][...] = total.astype(BF16)


def add_chips(kept, got):
    return pl.pallas_call(
        add_chips_kernel,
        out_shape=jax.ShapeDtypeStruct(kept.shape, BF16),
        in_specs=[vmem_spec()] * (1 + len(got)),
        out_specs=vmem_spec(),
        compiler_params=params(16),
        name="add_chips",
    )(kept, *got)


def ring(value, axis, step):
    return lax.ppermute(value, axis, [(i, (i + step) % 4) for i in range(4)])


def shards(activations, out_grads):
    where = jnp.stack([lax.axis_index(n) for n in ("row", "x", "z_hi", "y", "core")]).astype(jnp.int32)
    grads = out_grads[0]
    half = grads.shape[0] // 2

    turned = turn(where, activations[0])
    before = ring(grads, "z_hi", 1)
    after = ring(grads, "z_hi", -1)
    owns = [ring(grads, "x", -t) for t in (1, 2, 3)]
    near = jnp.concatenate([after, before])
    near, top, bottom, turned, *owns = lax.optimization_barrier((near, before[:half], after[half:], turned, *owns))

    inputs = lax.all_gather(turned, "row", axis=0)

    far_top = ring(top, "z_hi", 1)
    far_bottom = ring(bottom, "z_hi", -1)
    nears = [ring(near, "x", -t) for t in (1, 2, 3)]
    far_top, far_bottom, *nears = lax.optimization_barrier((far_top, far_bottom, *nears))

    far = jnp.concatenate([far_top, far_bottom])
    fars = [ring(far, "x", -t) for t in (1, 2, 3)]

    right = stage([grads, near, far] + [p for group in zip(owns, nears, fars) for p in group])
    other, mine = product(where, inputs, right)
    got = lax.ppermute(other, "core", [(0, 1), (1, 0)])
    kept, *sends = add_cores(where, mine, got)
    return add_chips(kept, [ring(sends[k - 1], "y", k) for k in (2, 1, 3)])


def solution(mesh):
    parts = Mesh(mesh.devices.reshape(4, 4, 4, 4, 2), ("row", "x", "z_hi", "y", "core"))
    in_specs = (P(("y", "core"), "row", ("x", "z_hi")), P(("y", "core"), ("x", "z_hi"), "row"))
    out_specs = P(("x", "z_hi", "y", "core"), "row")
    return jax.shard_map(shards, mesh=parts, in_specs=in_specs, out_specs=out_specs, check_vma=False)
```

```python
import jax
import jax.numpy as jnp
from jax import lax
from jax.experimental import pallas as pl
from jax.experimental.pallas import tpu as pltpu
from jax.sharding import Mesh, PartitionSpec as P

F32, BF16 = jnp.float32, jnp.bfloat16
CHUNK = 512


def vmem_spec():
    return pl.BlockSpec(memory_space=pltpu.VMEM)


def smem_spec():
    return pl.BlockSpec(memory_space=pltpu.SMEM)


def any_spec():
    return pl.BlockSpec(memory_space=pl.ANY)


def params(mib):
    return pltpu.CompilerParams(vmem_limit_bytes=mib << 20)


def turn_kernel(where, a_ref, out_ref, turned):
    h, core = where[2], where[4]
    share = out_ref.shape[0] // 8
    for q, ahead in enumerate((0, 1, 3, 2)):
        start = pl.multiple_of(lax.rem(h + ahead, 4) * 128, 128)
        turned[:, q * 128 : (q + 1) * 128] = a_ref[pl.ds(start, 128), :].T
    for y in range(4):
        for i, keeper in enumerate((1 - core, core)):
            at = pl.multiple_of((2 * y + keeper) * share, 32)
            out_ref[(4 * i + y) * share : (4 * i + y + 1) * share, :] = turned[pl.ds(at, share), :]


def turn(where, a):
    shape = (a.shape[1], a.shape[0])
    return pl.pallas_call(
        turn_kernel,
        out_shape=jax.ShapeDtypeStruct(shape, BF16),
        in_specs=[smem_spec(), vmem_spec()],
        out_specs=vmem_spec(),
        scratch_shapes=[pltpu.VMEM(shape, BF16)],
        compiler_params=params(16),
        name="turn",
    )(where, a)


def stage_kernel(where, own_ref, *refs):
    pieces, (out_ref, sems) = refs[:-2], refs[-2:]
    copies = []
    for t in range(4):
        chunk = lax.rem(where[1] + t, 4)
        at = t * CHUNK
        for i, ref in enumerate((own_ref.at[chunk], *pieces[2 * t : 2 * t + 2])):
            size = (128, 256, 128)[i]
            copies.append(pltpu.make_async_copy(ref, out_ref.at[pl.ds(at, size)], sems.at[t, i]))
            at += size
    for copy in copies:
        copy.start()
    for copy in copies:
        copy.wait()


def stage(where, owns, pieces):
    return pl.pallas_call(
        stage_kernel,
        out_shape=jax.ShapeDtypeStruct((4 * CHUNK, owns.shape[-1]), BF16),
        in_specs=[smem_spec()] + [any_spec()] * (1 + len(pieces)),
        out_specs=vmem_spec(),
        scratch_shapes=[pltpu.SemaphoreType.DMA((4, 3))],
        compiler_params=params(54),
        cost_estimate=pl.CostEstimate(flops=0, bytes_accessed=12 << 20, transcendentals=0),
        name="stage",
    )(where, owns, *pieces)


def product_kernel(where, a_ref, grads_ref, other_ref, own_ref, left, right, total, sems):
    waits = []
    for t in range(4):
        chunk = lax.rem(where[1] + t, 4)
        here = pl.ds(t * CHUNK, CHUNK)
        waits.append([
            pltpu.make_async_copy(a_ref.at[chunk], left.at[:, here], sems.at[t, 0]),
            pltpu.make_async_copy(grads_ref.at[here], right.at[here], sems.at[t, 1]),
        ])
    for copies in waits:
        for copy in copies:
            copy.start()
    share = other_ref.shape[1]
    for first, last in ((0, 1), (1, 2), (2, 4)):
        for copies in waits[first:last]:
            for copy in copies:
                copy.wait()
        across = slice(first * CHUNK, last * CHUNK)
        value = jnp.dot(left[:, across], right[across, :], preferred_element_type=F32)
        if first > 0:
            value = total[...] + value
        if last < 4:
            total[...] = value
        else:
            for y in range(4):
                other_ref[y] = value[y * share : (y + 1) * share].astype(BF16)
                own_ref[y] = value[(4 + y) * share : (5 + y) * share].astype(BF16)


def product(where, inputs, grads):
    rows, (tokens, columns) = inputs.shape[1], grads.shape
    return pl.pallas_call(
        product_kernel,
        out_shape=[jax.ShapeDtypeStruct((4, rows // 8, columns), BF16)] * 2,
        in_specs=[smem_spec(), any_spec(), any_spec()],
        out_specs=[vmem_spec(), vmem_spec()],
        scratch_shapes=[
            pltpu.VMEM((rows, tokens), BF16),
            pltpu.VMEM((tokens, columns), BF16),
            pltpu.VMEM((rows, columns), F32),
            pltpu.SemaphoreType.DMA((4, 2)),
        ],
        compiler_params=params(50),
        cost_estimate=pl.CostEstimate(flops=2 * rows * columns * tokens, bytes_accessed=12 << 20, transcendentals=0),
        name="product",
    )(where, inputs, grads)


def add_cores_kernel(where, own_ref, got_ref, *outs):
    y = where[3]
    for k in range(4):
        at = lax.rem(y + k, 4)
        outs[k][...] = (own_ref[at].astype(F32) + got_ref[at].astype(F32)).astype(outs[k].dtype)


def add_cores(where, own, got):
    shape = own.shape[1:]
    return pl.pallas_call(
        add_cores_kernel,
        out_shape=[jax.ShapeDtypeStruct(shape, F32)] + [jax.ShapeDtypeStruct(shape, BF16)] * 3,
        in_specs=[smem_spec(), vmem_spec(), vmem_spec()],
        out_specs=[vmem_spec()] * 4,
        compiler_params=params(16),
        name="add_cores",
    )(where, own, got)


def add_chips_kernel(kept_ref, *refs):
    total = kept_ref[...]
    for ref in refs[:-1]:
        total += ref[...].astype(F32)
    refs[-1][...] = total.astype(BF16)


def add_chips(kept, got):
    return pl.pallas_call(
        add_chips_kernel,
        out_shape=jax.ShapeDtypeStruct(kept.shape, BF16),
        in_specs=[vmem_spec()] * (1 + len(got)),
        out_specs=vmem_spec(),
        compiler_params=params(16),
        name="add_chips",
    )(kept, *got)


def ring(value, axis, step):
    return lax.ppermute(value, axis, [(i, (i + step) % 4) for i in range(4)])


def shards(activations, out_grads):
    where = jnp.stack([lax.axis_index(n) for n in ("row", "x", "z_hi", "y", "core")]).astype(jnp.int32)
    grads = out_grads[0]
    half = grads.shape[0] // 2

    turned = turn(where, activations[0])

    owns = lax.all_gather(grads, "x", axis=0)
    before = ring(grads, "z_hi", 1)
    after = ring(grads, "z_hi", -1)
    near = jnp.concatenate([after, before])
    near, top, bottom, turned = lax.optimization_barrier((near, before[:half], after[half:], turned))

    inputs = lax.all_gather(turned, "row", axis=0)

    far_top = ring(top, "z_hi", 1)
    far_bottom = ring(bottom, "z_hi", -1)
    nears = [ring(near, "x", -t) for t in (1, 2, 3)]
    far_top, far_bottom, *nears = lax.optimization_barrier((far_top, far_bottom, *nears))

    far = jnp.concatenate([far_top, far_bottom])
    fars = [ring(far, "x", -t) for t in (1, 2, 3)]

    right = stage(where, owns, [p for group in zip([near] + nears, [far] + fars) for p in group])
    other, mine = product(where, inputs, right)
    got = lax.ppermute(other, "core", [(0, 1), (1, 0)])
    kept, *sends = add_cores(where, mine, got)
    return add_chips(kept, [ring(sends[k - 1], "y", k) for k in (2, 1, 3)])


def solution(mesh):
    parts = Mesh(mesh.devices.reshape(4, 4, 4, 4, 2), ("row", "x", "z_hi", "y", "core"))
    in_specs = (P(("y", "core"), "row", ("x", "z_hi")), P(("y", "core"), ("x", "z_hi"), "row"))
    out_specs = P(("x", "z_hi", "y", "core"), "row")
    return jax.shard_map(shards, mesh=parts, in_specs=in_specs, out_specs=out_specs, check_vma=False)
```

```python
import jax
import jax.numpy as jnp
from jax import lax
from jax.experimental import pallas as pl
from jax.experimental.pallas import tpu as pltpu
from jax.sharding import Mesh, PartitionSpec as P

F32, BF16 = jnp.float32, jnp.bfloat16
CHUNK = 512


def vmem_spec():
    return pl.BlockSpec(memory_space=pltpu.VMEM)


def smem_spec():
    return pl.BlockSpec(memory_space=pltpu.SMEM)


def any_spec():
    return pl.BlockSpec(memory_space=pl.ANY)


def params(mib):
    return pltpu.CompilerParams(vmem_limit_bytes=mib << 20)


def turn_kernel(where, a_ref, out_ref, turned):
    h, core = where[2], where[4]
    share = out_ref.shape[0] // 8
    for q, ahead in enumerate((0, 1, 3, 2)):
        start = pl.multiple_of(lax.rem(h + ahead, 4) * 128, 128)
        turned[:, q * 128 : (q + 1) * 128] = a_ref[pl.ds(start, 128), :].T
    for y in range(4):
        for i, keeper in enumerate((1 - core, core)):
            at = pl.multiple_of((2 * y + keeper) * share, 32)
            out_ref[(4 * i + y) * share : (4 * i + y + 1) * share, :] = turned[pl.ds(at, share), :]


def turn(where, a):
    shape = (a.shape[1], a.shape[0])
    return pl.pallas_call(
        turn_kernel,
        out_shape=jax.ShapeDtypeStruct(shape, BF16),
        in_specs=[smem_spec(), vmem_spec()],
        out_specs=vmem_spec(),
        scratch_shapes=[pltpu.VMEM(shape, BF16)],
        compiler_params=params(16),
        name="turn",
    )(where, a)


def stage_kernel(*refs):
    pieces, (out_ref, sems) = refs[:-2], refs[-2:]
    at, copies = 0, []
    for i, ref in enumerate(pieces):
        copies.append(pltpu.make_async_copy(ref, out_ref.at[pl.ds(at, ref.shape[0])], sems.at[i]))
        at += ref.shape[0]
    for copy in copies:
        copy.start()
    for copy in copies:
        copy.wait()


def stage(pieces):
    tokens = sum(p.shape[0] for p in pieces)
    return pl.pallas_call(
        stage_kernel,
        out_shape=jax.ShapeDtypeStruct((tokens, pieces[0].shape[1]), BF16),
        in_specs=[any_spec()] * len(pieces),
        out_specs=vmem_spec(),
        scratch_shapes=[pltpu.SemaphoreType.DMA((len(pieces),))],
        compiler_params=params(54),
        cost_estimate=pl.CostEstimate(flops=0, bytes_accessed=12 << 20, transcendentals=0),
        name="stage",
    )(*pieces)


def product_kernel(where, a_ref, grads_ref, other_ref, own_ref, left, right, total, sems):
    waits = []
    for t in range(4):
        chunk = lax.rem(where[1] + t, 4)
        here = pl.ds(t * CHUNK, CHUNK)
        waits.append([
            pltpu.make_async_copy(a_ref.at[chunk], left.at[:, here], sems.at[t, 0]),
            pltpu.make_async_copy(grads_ref.at[here], right.at[here], sems.at[t, 1]),
        ])
    for copies in waits:
        for copy in copies:
            copy.start()
    share = other_ref.shape[1]
    for first, last in ((0, 1), (1, 2), (2, 4)):
        for copies in waits[first:last]:
            for copy in copies:
                copy.wait()
        across = slice(first * CHUNK, last * CHUNK)
        value = jnp.dot(left[:, across], right[across, :], preferred_element_type=F32)
        if first > 0:
            value = total[...] + value
        if last < 4:
            total[...] = value
        else:
            for y in range(4):
                other_ref[y] = value[y * share : (y + 1) * share].astype(BF16)
                own_ref[y] = value[(4 + y) * share : (5 + y) * share].astype(BF16)


def product(where, inputs, grads):
    rows, (tokens, columns) = inputs.shape[1], grads.shape
    return pl.pallas_call(
        product_kernel,
        out_shape=[jax.ShapeDtypeStruct((4, rows // 8, columns), BF16)] * 2,
        in_specs=[smem_spec(), any_spec(), any_spec()],
        out_specs=[vmem_spec(), vmem_spec()],
        scratch_shapes=[
            pltpu.VMEM((rows, tokens), BF16),
            pltpu.VMEM((tokens, columns), BF16),
            pltpu.VMEM((rows, columns), F32),
            pltpu.SemaphoreType.DMA((4, 2)),
        ],
        compiler_params=params(50),
        cost_estimate=pl.CostEstimate(flops=2 * rows * columns * tokens, bytes_accessed=12 << 20, transcendentals=0),
        name="product",
    )(where, inputs, grads)


def add_cores_kernel(where, own_ref, got_ref, *outs):
    y = where[3]
    for k in range(4):
        at = lax.rem(y + k, 4)
        outs[k][...] = (own_ref[at].astype(F32) + got_ref[at].astype(F32)).astype(outs[k].dtype)


def add_cores(where, own, got):
    shape = own.shape[1:]
    return pl.pallas_call(
        add_cores_kernel,
        out_shape=[jax.ShapeDtypeStruct(shape, F32)] + [jax.ShapeDtypeStruct(shape, BF16)] * 3,
        in_specs=[smem_spec(), vmem_spec(), vmem_spec()],
        out_specs=[vmem_spec()] * 4,
        compiler_params=params(16),
        name="add_cores",
    )(where, own, got)


def add_chips_kernel(kept_ref, *refs):
    total = kept_ref[...]
    for ref in refs[:-1]:
        total += ref[...].astype(F32)
    refs[-1][...] = total.astype(BF16)


def add_chips(kept, got):
    return pl.pallas_call(
        add_chips_kernel,
        out_shape=jax.ShapeDtypeStruct(kept.shape, BF16),
        in_specs=[vmem_spec()] * (1 + len(got)),
        out_specs=vmem_spec(),
        compiler_params=params(16),
        name="add_chips",
    )(kept, *got)


def ring(value, axis, step):
    return lax.ppermute(value, axis, [(i, (i + step) % 4) for i in range(4)])


def shards(activations, out_grads):
    where = jnp.stack([lax.axis_index(n) for n in ("row", "x", "z_hi", "y", "core")]).astype(jnp.int32)
    grads = out_grads[0]
    half = grads.shape[0] // 2

    turned = turn(where, activations[0])
    before = ring(grads, "z_hi", 1)
    after = ring(grads, "z_hi", -1)
    owns = [ring(grads, "x", -t) for t in (1, 2, 3)]
    near = jnp.concatenate([after, before])
    near, top, bottom, turned, *owns = lax.optimization_barrier((near, before[:half], after[half:], turned, *owns))

    inputs = lax.all_gather(turned, "row", axis=0)

    far_top = ring(top, "z_hi", 1)
    far_bottom = ring(bottom, "z_hi", -1)
    nears = [ring(near, "x", -t) for t in (1, 2, 3)]
    far_top, far_bottom, *nears = lax.optimization_barrier((far_top, far_bottom, *nears))

    far = jnp.concatenate([far_top, far_bottom])
    fars = [ring(far, "x", -t) for t in (1, 2, 3)]

    right = stage([grads, near, far] + [p for group in zip(owns, nears, fars) for p in group])
    other, mine = product(where, inputs, right)
    got = lax.ppermute(other, "core", [(0, 1), (1, 0)])
    kept, *sends = add_cores(where, mine, got)
    return add_chips(kept, [ring(sends[k - 1], "y", k) for k in (2, 3, 1)])


def solution(mesh):
    parts = Mesh(mesh.devices.reshape(4, 4, 4, 4, 2), ("row", "x", "z_hi", "y", "core"))
    in_specs = (P(("y", "core"), "row", ("x", "z_hi")), P(("y", "core"), ("x", "z_hi"), "row"))
    out_specs = P(("x", "z_hi", "y", "core"), "row")
    return jax.shard_map(shards, mesh=parts, in_specs=in_specs, out_specs=out_specs, check_vma=False)
```
